256 devices in a mesh: layer: 2 (over x_lo), wide: 16 (over z, x_hi), tp: 8 (over y, core).
Axes of the slice: x: 4 (x_hi: 2, x_lo: 2; x = x_hi * 2 + x_lo), y: 4, z: 8, core: 2. Of those that a mesh axis runs over, the one named last changes fastest.
Arguments:
- activations: bfloat16 [2048, 28672], P(('layer', 'wide'), 'tp'), parts along dimension 0, may hold values from -6 to 6
- grads_out: bfloat16 [16384, 1024], P(('layer', 'wide'), 'tp'), parts along dimension 0, may hold values from -6 to 6
- basis_in: bfloat16 [57344, 14336], P(('layer', 'tp'), 'wide'), parts along dimension 0, may hold values from -0.03125 to 0.03125
- basis_out: bfloat16 [16384, 8192], P(('layer', 'wide'), 'tp'), parts along dimension 0, may hold values from -0.0625 to 0.0625
- lengths: int32 [8], replicated, may hold values from 32 to 128, as said below
Outputs:
- eigenvalues: float32 [16384, 14336], P(('layer', 'tp'), 'wide'), parts along dimension 0
The draws below stay inside these ranges and needn't reach their ends.
There are 2 independent parts, one for each index of `layer`. The reference program is written for one: setup_inputs(seed, part) draws one part's arguments, and reference() takes and returns one part's arrays. A program takes and returns all parts, laid end to end along the dimension named above; an argument that names none is the same for every part. Nothing has to cross between parts.
Inputs may be any that keep to these rules, and one draw needn't show every extreme that they name: `lengths`: every draw has a sequence with all 128 tokens live.
All inputs are finite; a program needn't handle non-finite values.
Results may differ from the reference program's by a relative error of at most 0.0029.
Values may be sent and summed in bfloat16 or wider, within the bound.
No kernel may reach another device: no remote copies, remote signals or barrier semaphores. Data moves between devices by JAX's collectives and lax.ppermute only.
A program may use at most 64 MiB of HBM per device.

```python
import jax
import jax.numpy as jnp
from jax import lax

DIN = 28672
DOUT = 8192
KA = 14336
LEN = 128
SEQS = 8
TOKENS = 1024


def draw_lengths(key, part):
    key = jax.random.fold_in(key, 11)
    values = jax.random.randint(key, (SEQS,), LEN // 4, LEN + 1)
    chosen = jax.random.randint(jax.random.fold_in(key, 1), (), 0, SEQS)
    return jnp.where(jnp.arange(SEQS) == chosen, LEN, values).astype(jnp.int32)


def steps_of(rng, extent, split, low, top_value):
    def one(position, parts):
        heights = jax.random.uniform(jax.random.fold_in(jax.random.fold_in(rng, 6), position), (parts,), jnp.float32, low / len(split), top_value / len(split))
        return jnp.repeat(jnp.exp(heights), extent[position] // parts).reshape((-1,) + (1,) * (len(extent) - position - 1))

    gain = one(*split[0])
    for cut in split[1:]:
        gain = gain * one(*cut)
    return gain


def noise(rng, dims, width, reach, cuts=(), kind=jnp.bfloat16):
    factor_of = steps_of(rng, dims, cuts, -0.22, 0.18) if cuts else 1.0
    result = jax.random.normal(rng, dims, jnp.float32) * width * factor_of
    return jnp.minimum(jnp.maximum(result, -reach), reach).astype(kind)


def setup_inputs(seed: int = 0, part: int = 0) -> dict:
    keys = jax.random.split(jax.random.key(seed), 6)
    own_keys = jax.random.split(jax.random.fold_in(keys[5], part), 6)
    return {
        "activations": noise(own_keys[0], (TOKENS, DIN), 1.0, 6.0, ((0, 16), (1, 8))),
        "grads_out": noise(own_keys[1], (DOUT, TOKENS), 1.0, 6.0, ((0, 16), (1, 8))),
        "basis_in": noise(own_keys[2], (DIN, KA), DIN ** -0.5, 0.03125, ((0, 8), (1, 16))),
        "basis_out": noise(own_keys[3], (DOUT, DOUT), DOUT ** -0.5, 0.0625, ((0, 16), (1, 8))),
        "lengths": draw_lengths(jax.random.fold_in(keys[5], 71), part),
    }


def reference(activations, grads_out, basis_in, basis_out, lengths):
    token_index = jnp.arange(TOKENS, dtype=jnp.int32)
    live_mask = (token_index % LEN) < lengths[token_index // LEN]
    masked = grads_out * live_mask[None, :].astype(jnp.bfloat16)
    rotated_in = jnp.dot(activations, basis_in, preferred_element_type=jnp.float32).astype(jnp.bfloat16)
    rotated_out = jnp.dot(masked.T, basis_out, preferred_element_type=jnp.float32).astype(jnp.bfloat16)

    def accumulate(running, sequence):
        offset = (sequence * LEN).astype(jnp.int32)
        outer_side = lax.dynamic_slice_in_dim(rotated_out, offset, LEN, 0)
        inner_side = lax.dynamic_slice_in_dim(rotated_in, offset, LEN, 0)
        product = jnp.dot(outer_side.T, inner_side, preferred_element_type=jnp.float32)
        return running + product * product, None

    summed = lax.scan(accumulate, jnp.zeros((DOUT, KA), jnp.float32), jnp.arange(SEQS, dtype=jnp.int32))[0]
    return summed / jnp.sum(lengths).astype(jnp.float32)
```

```python
import jax
import jax.numpy as jnp
from jax import lax
from jax.experimental import pallas as pl
from jax.experimental.pallas import tpu as pltpu
from jax.sharding import PartitionSpec as P

LEN = 128
SEQS = 8
HALF = LEN // 2
Z = 8
RS_DTYPE = jnp.bfloat16


def shift_z(x, step):
    pairs = [(z * 2 + h, (z + step) % Z * 2 + h) for z in range(Z) for h in range(2)]
    return lax.ppermute(x, "wide", pairs)


def swap_x(x):
    return lax.ppermute(x, "wide", [(i, i ^ 1) for i in range(2 * Z)])


def spread(x):
    copies = jnp.broadcast_to(x[None], (8,) + x.shape)
    return lax.all_to_all(copies, "tp", 0, 0, tiled=True)


def after(values, *others):
    return lax.optimization_barrier((values, others))[0]


def partial_out_kernel(order, g_ref, b_ref, o_ref):
    o_ref[0] = lax.dot_general(
        g_ref[0], b_ref[...], (((0,), (0,)), ((), ())), preferred_element_type=jnp.float32
    ).astype(o_ref.dtype)


def partial_out(order, grads, basis):
    _, rows, _ = grads.shape
    cols = basis.shape[1]
    return pl.pallas_call(
        partial_out_kernel,
        out_shape=jax.ShapeDtypeStruct((SEQS, LEN, cols), jnp.float32),
        grid_spec=pltpu.PrefetchScalarGridSpec(
            num_scalar_prefetch=1,
            grid=(SEQS,),
            in_specs=[
                pl.BlockSpec((1, rows, LEN), lambda k, order: (order[k], 0, 0)),
                pl.BlockSpec((rows, cols), lambda k, order: (0, 0)),
            ],
            out_specs=pl.BlockSpec((1, LEN, cols), lambda k, order: (k, 0, 0)),
        ),
        cost_estimate=pl.CostEstimate(
            flops=2 * SEQS * LEN * rows * cols, bytes_accessed=8 * 2**20, transcendentals=0
        ),
    )(order, grads, basis)


def rotate_in(blocks, basis):
    rows = jnp.concatenate(blocks, axis=0)
    return jnp.dot(rows, basis, preferred_element_type=jnp.float32)


def scatter_sum(partial):
    tokens, cols = partial.shape
    pieces = lax.all_to_all(partial.reshape(8, tokens // 8, cols), "tp", 0, 0, tiled=True)
    return jnp.sum(pieces, axis=0).astype(jnp.bfloat16)


def products_kernel(count, *refs):
    scale_ref, base_ref = refs[0], refs[1]
    outs, ins = refs[2 : 2 + 2 * count], refs[2 + 2 * count : 2 + 4 * count]
    o_ref = refs[-1]
    total = base_ref[...] if base_ref is not None else None
    for n in range(count):
        left = jnp.concatenate([outs[2 * n][...], outs[2 * n + 1][...]], axis=0)
        right = jnp.concatenate([ins[2 * n][...], ins[2 * n + 1][...]], axis=0)
        product = lax.dot_general(
            left, right, (((0,), (0,)), ((), ())), preferred_element_type=jnp.float32
        )
        total = product * product if total is None else total + product * product
    if scale_ref is not None:
        total = total / scale_ref[0]
    o_ref[...] = total


def products(base, pairs, scale=None):
    out_cols = pairs[0][0][0].shape[1]
    in_cols = pairs[0][1][0].shape[1]
    tile = 128
    count = len(pairs)
    outs = [block for pair in pairs for block in pair[0]]
    ins = [block for pair in pairs for block in pair[1]]
    args, specs = [], []
    if scale is not None:
        args.append(scale.reshape(1))
        specs.append(pl.BlockSpec(memory_space=pltpu.SMEM))
    if base is not None:
        args.append(base)
        specs.append(pl.BlockSpec((tile, in_cols), lambda i: (i, 0)))
    args += outs + ins
    specs += [pl.BlockSpec((HALF, tile), lambda i: (0, i))] * len(outs)
    specs += [pl.BlockSpec((HALF, in_cols), lambda i: (0, 0))] * len(ins)

    def kernel(*refs):
        refs = list(refs)
        scale_ref = refs.pop(0) if scale is not None else None
        base_ref = refs.pop(0) if base is not None else None
        products_kernel(count, scale_ref, base_ref, *refs)

    return pl.pallas_call(
        kernel,
        out_shape=jax.ShapeDtypeStruct((out_cols, in_cols), jnp.float32),
        grid=(out_cols // tile,),
        in_specs=specs,
        out_specs=pl.BlockSpec((tile, in_cols), lambda i: (i, 0)),
        compiler_params=pltpu.CompilerParams(vmem_limit_bytes=32 * 2**20),
        cost_estimate=pl.CostEstimate(
            flops=4 * count * LEN * out_cols * in_cols, bytes_accessed=8 * 2**20, transcendentals=0
        ),
    )(*args)


def on_device(activations, grads_out, basis_in, basis_out, lengths):
    place = lax.axis_index("wide")
    z, h = place // 2, place % 2
    order = (z + lax.iota(jnp.int32, SEQS)) % SEQS

    a, c = {}, {}
    a[0] = activations
    a[-1], a[1], c[0] = shift_z(a[0], 1), shift_z(a[0], -1), swap_x(a[0])
    grads = spread(grads_out)
    a[-1], a[1], c[0], grads = lax.optimization_barrier((a[-1], a[1], c[0], grads))

    a[-2], a[2], c[1] = shift_z(a[-1], 1), shift_z(a[1], -1), swap_x(a[1])
    part = partial_out(order, grads, basis_out)
    send_p, send_m = part[4].astype(RS_DTYPE), part[5].astype(RS_DTYPE)
    rs_p, rs_m = shift_z(send_p, 1), shift_z(send_m, -1)
    in1 = rotate_in([a[0], c[0], a[1], a[-1]], after(basis_in, send_p, send_m))
    a[-2], a[2], c[1], rs_p, rs_m, in1 = lax.optimization_barrier((a[-2], a[2], c[1], rs_p, rs_m, in1))

    a[-3], a[3], c[2] = shift_z(a[-2], 1), shift_z(a[2], -1), swap_x(a[2])
    send_p = (rs_p.astype(jnp.float32) + part[3]).astype(RS_DTYPE)
    send_m = (rs_m.astype(jnp.float32) + part[6]).astype(RS_DTYPE)
    rs_p, rs_m = shift_z(send_p, 1), shift_z(send_m, -1)
    sum1 = scatter_sum(in1)
    in2 = rotate_in([a[-2], a[2], c[1]], after(basis_in, send_p, send_m))
    a[-3], a[3], c[2], rs_p, rs_m, sum1, in2 = lax.optimization_barrier(
        (a[-3], a[3], c[2], rs_p, rs_m, sum1, in2)
    )

    a[4], c[3], c[-2] = shift_z(a[-3], 1), shift_z(c[2], -1), swap_x(a[-2])
    send_p = (rs_p.astype(jnp.float32) + part[2]).astype(RS_DTYPE)
    send_m = (rs_m.astype(jnp.float32) + part[7]).astype(RS_DTYPE)
    rs_p, rs_m = shift_z(send_p, 1), shift_z(send_m, -1)
    all1 = spread(sum1)
    in3 = rotate_in([a[-3], a[3], c[2]], after(basis_in, send_p, send_m))
    a[4], c[3], c[-2], rs_p, rs_m, all1, in3 = lax.optimization_barrier(
        (a[4], c[3], c[-2], rs_p, rs_m, all1, in3)
    )

    c[-3], c[4], c[-1] = shift_z(c[-2], 1), shift_z(c[3], -1), swap_x(a[-1])
    send_p = (rs_p.astype(jnp.float32) + part[1]).astype(RS_DTYPE)
    own = part[0] + rs_m.astype(jnp.float32)
    rs_p = shift_z(send_p, 1)
    sum23 = scatter_sum(jnp.concatenate([in2, in3], axis=0))
    in4 = rotate_in([a[4], c[3], c[-2]], after(basis_in, send_p, own))
    c[-3], c[4], c[-1], rs_p, sum23, in4 = lax.optimization_barrier((c[-3], c[4], c[-1], rs_p, sum23, in4))

    own = own + rs_p.astype(jnp.float32)
    cols = own.shape[1]
    mine = lax.dynamic_slice(own, (h * HALF, 0), (HALF, cols))
    theirs = lax.dynamic_slice(own, ((1 - h) * HALF, 0), (HALF, cols))
    got = swap_x(theirs)
    in5 = rotate_in([c[-3], c[4], c[-1]], after(basis_in, theirs))
    token = lax.iota(jnp.int32, HALF) + h * HALF
    live = token < lax.dynamic_index_in_dim(lengths, z, 0, keepdims=False)
    b, d = {}, {}
    b[0] = jnp.where(live[:, None], mine + got, 0.0).astype(jnp.bfloat16)
    b[0], in5 = lax.optimization_barrier((b[0], in5))

    b[-1], b[1], d[0] = shift_z(b[0], 1), shift_z(b[0], -1), swap_x(b[0])
    sum45 = scatter_sum(jnp.concatenate([in4, in5], axis=0))
    all23 = spread(sum23)
    b[-1], b[1], d[0] = lax.optimization_barrier((b[-1], b[1], d[0]))
    b[-2], b[2], d[1] = shift_z(b[-1], 1), shift_z(b[1], -1), swap_x(b[1])
    b[-2], b[2], d[1], sum45, all23 = lax.optimization_barrier((b[-2], b[2], d[1], sum45, all23))
    all45 = spread(sum45)
    b[-3], b[3], d[2] = shift_z(b[-2], 1), shift_z(b[2], -1), swap_x(b[2])
    b[-3], b[3], d[2] = lax.optimization_barrier((b[-3], b[3], d[2]))
    b[4], d[3], d[-2] = shift_z(b[-3], 1), shift_z(d[2], -1), swap_x(b[-2])
    b[4], d[3], d[-2] = lax.optimization_barrier((b[4], d[3], d[-2]))
    d[-3], d[4], d[-1] = shift_z(d[-2], 1), shift_z(d[3], -1), swap_x(b[-1])

    ins = {}
    wide = basis_in.shape[1]
    first = all1.reshape(4, HALF, wide)
    second = all23.reshape(6, HALF, wide)
    third = all45.reshape(6, HALF, wide)
    ia = {0: first[0], 1: first[2], -1: first[3], -2: second[0], 2: second[1], -3: second[3], 3: second[4], 4: third[0]}
    ic = {0: first[1], 1: second[2], 2: second[5], 3: third[1], -2: third[2], -3: third[3], 4: third[4], -1: third[5]}
    pair = lambda k: ((b[k], d[k]), (ia[k], ic[k]))
    total = jnp.sum(lengths).astype(jnp.float32)
    early = products(None, [pair(0), pair(1), pair(2)])
    return products(early, [pair(3), pair(-2), pair(-3), pair(4), pair(-1)], total)


def solution(mesh):
    placed = (
        P(("layer", "wide"), "tp"),
        P(("layer", "wide"), "tp"),
        P(("layer", "tp"), "wide"),
        P(("layer", "wide"), "tp"),
        P(),
    )
    return jax.shard_map(
        on_device, mesh=mesh, in_specs=placed, out_specs=P(("layer", "tp"), "wide"), check_vma=False
    )
```

```python
import functools

import jax
import jax.numpy as jnp
from jax import lax
from jax.experimental import pallas as pl
from jax.experimental.pallas import tpu as pltpu
from jax.sharding import PartitionSpec as P

LEN = 128
SEQS = 8
HALF = LEN // 2
Z = 8
Y = 4
SEND = jnp.bfloat16
ALONG_Z = [[2 * z + h for z in range(Z)] for h in range(2)]
QUICK = pl.CostEstimate(flops=1, bytes_accessed=1, transcendentals=0)
VMEM_LIMIT = 48 * 2**20


def shift_z(x, step):
    pairs = [(z * 2 + h, (z + step) % Z * 2 + h) for z in range(Z) for h in range(2)]
    return lax.ppermute(x, "wide", pairs)


def swap_x(x):
    return lax.ppermute(x, "wide", [(i, i ^ 1) for i in range(2 * Z)])


def shift_y(x, step):
    pairs = [(y * 2 + c, (y + step) % Y * 2 + c) for y in range(Y) for c in range(2)]
    return lax.ppermute(x, "tp", pairs)


def swap_core(x):
    return lax.ppermute(x, "tp", [(i, i ^ 1) for i in range(2 * Y)])


def along_z(x):
    return lax.all_to_all(x, "wide", 0, 0, tiled=True, axis_index_groups=ALONG_Z)


def together(*values):
    return lax.optimization_barrier(values)


def rotate_kernel(count, core_ref, *refs):
    blocks, basis_ref = refs[:count], refs[count]
    mine_ref, theirs_ref, total = refs[count + 1 :]
    rows = jnp.concatenate([block[...] for block in blocks], axis=0)
    term = jnp.dot(rows, basis_ref[...], preferred_element_type=jnp.float32)

    @pl.when(pl.program_id(0) == 0)
    def _():
        total[...] = term

    @pl.when(pl.program_id(0) == 1)
    def _():
        total[...] += term
        half = count * HALF // 2
        core = core_ref[0]
        mine_ref[...] = total[pl.ds(pl.multiple_of(core * half, 16), half), :]
        theirs_ref[...] = total[pl.ds(pl.multiple_of((1 - core) * half, 16), half), :]


def rotate_in(blocks, basis, core):
    count = len(blocks)
    depth, cols = basis.shape
    tile = depth // 2
    half = count * HALF // 2
    shape = jax.ShapeDtypeStruct((half, cols), jnp.float32)
    whole = pl.BlockSpec((half, cols), lambda k, core: (0, 0))
    return pl.pallas_call(
        functools.partial(rotate_kernel, count),
        out_shape=(shape, shape),
        grid_spec=pltpu.PrefetchScalarGridSpec(
            num_scalar_prefetch=1,
            grid=(2,),
            in_specs=[pl.BlockSpec((HALF, tile), lambda k, core: (0, k))] * count
            + [pl.BlockSpec((tile, cols), lambda k, core: (k, 0))],
            out_specs=(whole, whole),
            scratch_shapes=[pltpu.VMEM((count * HALF, cols), jnp.float32)],
        ),
        compiler_params=pltpu.CompilerParams(vmem_limit_bytes=VMEM_LIMIT),
        cost_estimate=QUICK,
    )(core, *blocks, basis)


def partial_kernel(place_ref, *refs):
    grads, (near_ref, far_ref, out_ref) = refs[:4], refs[4:]
    y, core = place_ref[0], place_ref[1]
    rows = near_ref.shape[0]
    lefts = []
    for near, far in (grads[:2], grads[2:]):
        for k in range(Y):
            part = pl.ds(k * rows, rows)
            lefts.append(jnp.concatenate([near[part, :], far[part, :]], axis=0))
    left = jnp.concatenate(lefts, axis=1)
    right = jnp.concatenate([near_ref[...], far_ref[...]], axis=0)
    term = lax.dot_general(left, right, (((0,), (0,)), ((), ())), preferred_element_type=jnp.float32)
    for n in range(SEQS):
        owner = jnp.where(n < Y, core, 1 - core)
        sequence = 2 * lax.rem(y + n % Y, Y) + owner
        out_ref[sequence] = term[n * LEN : (n + 1) * LEN, :].astype(out_ref.dtype)


def partial_out(grads, near, far, place):
    cols = near.shape[1]
    vmem = pl.BlockSpec(memory_space=pltpu.VMEM)
    return pl.pallas_call(
        partial_kernel,
        out_shape=jax.ShapeDtypeStruct((SEQS, LEN, cols), SEND),
        in_specs=[pl.BlockSpec(memory_space=pltpu.SMEM)] + [vmem] * 6,
        out_specs=vmem,
        compiler_params=pltpu.CompilerParams(vmem_limit_bytes=VMEM_LIMIT),
        cost_estimate=QUICK,
    )(place, *grads, near, far)


def split_kernel(place_ref, mine_ref, got_ref, *outs):
    rows = outs[0].shape[0]
    place = place_ref[0]
    for k, out in enumerate(outs):
        start = pl.multiple_of(lax.rem(place + k, Y) * rows, 16)
        out[...] = mine_ref[pl.ds(start, rows), :] + got_ref[pl.ds(start, rows), :]


def split_sum(mine, got, place):
    half, cols = mine.shape
    shape = jax.ShapeDtypeStruct((half // Y, cols), jnp.float32)
    return pl.pallas_call(
        split_kernel,
        out_shape=(shape,) * Y,
        in_specs=[pl.BlockSpec(memory_space=pltpu.SMEM)] + [pl.BlockSpec(memory_space=pltpu.VMEM)] * 2,
        out_specs=(pl.BlockSpec(memory_space=pltpu.VMEM),) * Y,
        compiler_params=pltpu.CompilerParams(vmem_limit_bytes=VMEM_LIMIT),
    )(place, mine, got)


def join_kernel(place_ref, *refs):
    pieces, out = refs[:Y], refs[Y]
    rows = pieces[0].shape[0]
    for k, piece in enumerate(pieces):
        start = pl.multiple_of(lax.rem(place_ref[0] + k, Y) * rows, 16)
        out[pl.ds(start, rows), :] = piece[...]


def join(pieces, place):
    rows, cols = pieces[0].shape
    return pl.pallas_call(
        join_kernel,
        out_shape=jax.ShapeDtypeStruct((Y * rows, cols), pieces[0].dtype),
        in_specs=[pl.BlockSpec(memory_space=pltpu.SMEM)] + [pl.BlockSpec(memory_space=pltpu.VMEM)] * Y,
        out_specs=pl.BlockSpec(memory_space=pltpu.VMEM),
        compiler_params=pltpu.CompilerParams(vmem_limit_bytes=VMEM_LIMIT),
    )(place, *pieces)


def products_kernel(layout, place_ref, scale_ref, *refs):
    outs_ref, refs = refs[0], refs[1:]
    chunks = len(layout)
    halves, o_ref, rows = refs[: 2 * chunks], refs[-2], refs[-1]
    z, h, core = place_ref[0], place_ref[1], place_ref[2]

    @pl.when(pl.program_id(0) == 0)
    def _():
        for n, blocks in enumerate(layout):
            for other in range(2):
                source = halves[2 * n + other]
                first = core if other == 0 else 1 - core
                count = len(blocks) // 2
                for slot in range(count):
                    low, high = blocks[slot], blocks[count + slot]
                    index = jnp.where(first == 0, low[0], high[0])
                    side = jnp.where(first == 0, low[1], high[1])
                    half = jnp.where(side == 0, h, 1 - h)
                    start = pl.multiple_of(index * LEN + half * HALF, 16)
                    rows[pl.ds(start, HALF), :] = source[slot * HALF : (slot + 1) * HALF, :]

    total = None
    for n in range(SEQS):
        product = lax.dot_general(
            outs_ref[lax.rem(z + n, SEQS), 0],
            rows[n * LEN : (n + 1) * LEN, :],
            (((0,), (0,)), ((), ())),
            preferred_element_type=jnp.float32,
        )
        total = product * product if total is None else total + product * product
    o_ref[...] = total / scale_ref[0]


def products(rotated_out, chunks, layout, place, scale):
    _, _, _, half_cols = rotated_out.shape
    in_cols = chunks[0][0].shape[1]
    tile = 256
    per = half_cols // tile
    halves = [half for chunk in chunks for half in chunk]
    smem = pl.BlockSpec(memory_space=pltpu.SMEM)
    return pl.pallas_call(
        functools.partial(products_kernel, layout),
        out_shape=jax.ShapeDtypeStruct((2 * half_cols, in_cols), jnp.float32),
        grid=(2 * per,),
        in_specs=[smem, smem, pl.BlockSpec((SEQS, 1, LEN, tile), lambda i: (0, i // per, 0, i % per))]
        + [pl.BlockSpec(half.shape, lambda i: (0, 0)) for half in halves],
        out_specs=pl.BlockSpec((tile, in_cols), lambda i: (i, 0)),
        scratch_shapes=[pltpu.VMEM((SEQS * LEN, in_cols), jnp.bfloat16)],
        compiler_params=pltpu.CompilerParams(vmem_limit_bytes=VMEM_LIMIT),
        cost_estimate=QUICK,
    )(place, scale.reshape(1), rotated_out, *halves)


def scatter_y(mine, theirs, place):
    own, *away = split_sum(mine, swap_core(theirs), place)
    return own, [shift_y(piece, k + 1) for k, piece in enumerate(away)]


def gather_y(own, came, place):
    piece = (own + came[0] + came[1] + came[2]).astype(jnp.bfloat16)
    return join([piece] + [shift_y(piece, -k) for k in (1, 2, 3)], place)


def on_device(activations, grads_out, basis_in, basis_out, lengths):
    wide, tp = lax.axis_index("wide"), lax.axis_index("tp")
    z, h = wide // 2, wide % 2
    y, core = tp // 2, tp % 2
    place, core_at = y.reshape(1), core.reshape(1)
    rows, out_cols = basis_out.shape
    half_cols = out_cols // 2

    a, c = {}, {}
    a[0] = activations
    a[-1], a[1] = shift_z(a[0], 1), shift_z(a[0], -1)
    far = swap_x(lax.dynamic_slice(basis_out, (0, (1 - h) * half_cols), (rows, half_cols)))
    near = lax.dynamic_slice(basis_out, (0, h * half_cols), (rows, half_cols))
    grads = [grads_out] + [shift_y(grads_out, -k) for k in (1, 2, 3)]
    a[-1], a[1], near, far, *grads = together(a[-1], a[1], near, far, *grads)

    a[-2], a[2] = shift_z(a[-1], 1), shift_z(a[1], -1)
    grads_near = jnp.concatenate(grads, axis=0)
    grads_far = swap_x(grads_near)
    a[-2], a[2], grads_near, grads_far = together(a[-2], a[2], grads_near, grads_far)

    a[-3], a[3], c[2] = shift_z(a[-2], 1), shift_z(a[2], -1), swap_x(a[2])
    grads = [grads_near, grads_far, swap_core(grads_near), swap_core(grads_far)]
    part = partial_out(grads, near, far, jnp.stack([y, core]))
    a[-3], a[3], c[2], part, a[1], a[-2], a[-1], a[0], basis_in = together(
        a[-3], a[3], c[2], part, a[1], a[-2], a[-1], a[0], basis_in
    )

    first = [(0, 0), (1, 0), (2, 0), (3, 0), (-1, 0), (-2, 0), (-3, 0), (2, 1)]
    second = [(4, 0), (1, 1), (0, 1), (-2, 1), (-1, 1), (3, 1), (-3, 1), (4, 1)]
    block = lambda at: (a, c)[at[1]][at[0]]
    summands = along_z(part)
    a[4], c[3] = shift_z(a[-3], 1), shift_z(c[2], -1)
    c[-2], c[1], c[0], c[-1] = swap_x(a[-2]), swap_x(a[1]), swap_x(a[0]), swap_x(a[-1])
    c[-3], c[4] = shift_z(c[-2], 1), shift_z(c[3], -1)
    mine_a, theirs_a = rotate_in([block(at) for at in first], basis_in, core_at)
    a[4], c[-3], c[4], c[1], c[-1], c[0], summands, mine_a, theirs_a, basis_in = together(
        a[4], c[-3], c[4], c[1], c[-1], c[0], summands, mine_a, theirs_a, basis_in
    )

    token = lax.iota(jnp.int32, LEN)
    live = token < lax.dynamic_index_in_dim(lengths, z, 0, keepdims=False)
    summed = jnp.sum(summands.astype(jnp.float32), axis=0)
    summed = jnp.where(live[:, None], summed, 0.0).astype(jnp.bfloat16)
    copies = jnp.broadcast_to(summed[None], (2 * Z,) + summed.shape)
    copies, basis_in, theirs_a = together(copies, basis_in, theirs_a)
    rotated_out = lax.all_to_all(copies, "wide", 0, 0, tiled=True)
    own_a, came_a = scatter_y(mine_a, theirs_a, place)

    mine_b, theirs_b = rotate_in([block(at) for at in second], basis_in, core_at)
    own_b, came_b = scatter_y(mine_b, theirs_b, place)
    rows_a = gather_y(own_a, came_a, place)
    chunk_a = (rows_a, swap_core(rows_a))
    rows_b = gather_y(own_b, came_b, place)
    chunk_b = (rows_b, swap_core(rows_b))
    scale = jnp.sum(lengths).astype(jnp.float32)
    layout = [[(k % SEQS, side) for k, side in blocks] for blocks in (first, second)]
    rotated_out = rotated_out.reshape(SEQS, 2, LEN, half_cols)
    return products(rotated_out, [chunk_a, chunk_b], layout, jnp.stack([z, h, core]), scale)


def solution(mesh):
    placed = (
        P(("layer", "wide"), "tp"),
        P(("layer", "wide"), "tp"),
        P(("layer", "tp"), "wide"),
        P(("layer", "wide"), "tp"),
        P(),
    )
    return jax.shard_map(
        on_device, mesh=mesh, in_specs=placed, out_specs=P(("layer", "tp"), "wide"), check_vma=False
    )
```

```python
import functools

import jax
import jax.numpy as jnp
from jax import lax
from jax.experimental import pallas as pl
from jax.experimental.pallas import tpu as pltpu
from jax.sharding import PartitionSpec as P

LEN = 128
SEQS = 8
HALF = LEN // 2
Z = 8
Y = 4
SEND = jnp.bfloat16
ALONG_Z = [[2 * z + h for z in range(Z)] for h in range(2)]
QUICK = pl.CostEstimate(flops=1, bytes_accessed=1, transcendentals=0)
VMEM_LIMIT = 48 * 2**20


def shift_z(x, step):
    pairs = [(z * 2 + h, (z + step) % Z * 2 + h) for z in range(Z) for h in range(2)]
    return lax.ppermute(x, "wide", pairs)


def swap_x(x):
    return lax.ppermute(x, "wide", [(i, i ^ 1) for i in range(2 * Z)])


def shift_y(x, step):
    pairs = [(y * 2 + c, (y + step) % Y * 2 + c) for y in range(Y) for c in range(2)]
    return lax.ppermute(x, "tp", pairs)


def swap_core(x):
    return lax.ppermute(x, "tp", [(i, i ^ 1) for i in range(2 * Y)])


def along_z(x):
    return lax.all_to_all(x, "wide", 0, 0, tiled=True, axis_index_groups=ALONG_Z)


def together(*values):
    return lax.optimization_barrier(values)


def rotate_kernel(count, core_ref, *refs):
    blocks, basis_ref = refs[:count], refs[count]
    mine_ref, theirs_ref, total = refs[count + 1 :]
    rows = jnp.concatenate([block[...] for block in blocks], axis=0)
    term = jnp.dot(rows, basis_ref[...], preferred_element_type=jnp.float32)

    @pl.when(pl.program_id(0) == 0)
    def _():
        total[...] = term

    @pl.when(pl.program_id(0) == 1)
    def _():
        total[...] += term
        half = count * HALF // 2
        core = core_ref[0]
        mine_ref[...] = total[pl.ds(pl.multiple_of(core * half, 16), half), :]
        theirs_ref[...] = total[pl.ds(pl.multiple_of((1 - core) * half, 16), half), :]


def rotate_in(blocks, basis, core):
    count = len(blocks)
    depth, cols = basis.shape
    tile = depth // 2
    half = count * HALF // 2
    shape = jax.ShapeDtypeStruct((half, cols), jnp.float32)
    whole = pl.BlockSpec((half, cols), lambda k, core: (0, 0))
    return pl.pallas_call(
        functools.partial(rotate_kernel, count),
        out_shape=(shape, shape),
        grid_spec=pltpu.PrefetchScalarGridSpec(
            num_scalar_prefetch=1,
            grid=(2,),
            in_specs=[pl.BlockSpec((HALF, tile), lambda k, core: (0, k))] * count
            + [pl.BlockSpec((tile, cols), lambda k, core: (k, 0))],
            out_specs=(whole, whole),
            scratch_shapes=[pltpu.VMEM((count * HALF, cols), jnp.float32)],
        ),
        compiler_params=pltpu.CompilerParams(vmem_limit_bytes=VMEM_LIMIT),
        cost_estimate=QUICK,
    )(core, *blocks, basis)


def partial_kernel(place_ref, *refs):
    grads, (near_ref, far_ref, out_ref) = refs[:4], refs[4:]
    y, core = place_ref[0], place_ref[1]
    rows = near_ref.shape[0]
    lefts = []
    for near, far in (grads[:2], grads[2:]):
        for k in range(Y):
            part = pl.ds(k * rows, rows)
            lefts.append(jnp.concatenate([near[part, :], far[part, :]], axis=0))
    left = jnp.concatenate(lefts, axis=1)
    right = jnp.concatenate([near_ref[...], far_ref[...]], axis=0)
    term = lax.dot_general(left, right, (((0,), (0,)), ((), ())), preferred_element_type=jnp.float32)
    for n in range(SEQS):
        owner = jnp.where(n < Y, core, 1 - core)
        sequence = 2 * lax.rem(y + n % Y, Y) + owner
        out_ref[sequence] = term[n * LEN : (n + 1) * LEN, :].astype(out_ref.dtype)


def partial_out(grads, near, far, place):
    cols = near.shape[1]
    vmem = pl.BlockSpec(memory_space=pltpu.VMEM)
    return pl.pallas_call(
        partial_kernel,
        out_shape=jax.ShapeDtypeStruct((SEQS, LEN, cols), SEND),
        in_specs=[pl.BlockSpec(memory_space=pltpu.SMEM)] + [vmem] * 6,
        out_specs=vmem,
        compiler_params=pltpu.CompilerParams(vmem_limit_bytes=VMEM_LIMIT),
        cost_estimate=QUICK,
    )(place, *grads, near, far)


def split_kernel(place_ref, mine_ref, got_ref, *outs):
    rows = outs[0].shape[0]
    place = place_ref[0]
    for k, out in enumerate(outs):
        start = pl.multiple_of(lax.rem(place + k, Y) * rows, 16)
        out[...] = mine_ref[pl.ds(start, rows), :] + got_ref[pl.ds(start, rows), :]


def split_sum(mine, got, place):
    half, cols = mine.shape
    shape = jax.ShapeDtypeStruct((half // Y, cols), jnp.float32)
    return pl.pallas_call(
        split_kernel,
        out_shape=(shape,) * Y,
        in_specs=[pl.BlockSpec(memory_space=pltpu.SMEM)] + [pl.BlockSpec(memory_space=pltpu.VMEM)] * 2,
        out_specs=(pl.BlockSpec(memory_space=pltpu.VMEM),) * Y,
        compiler_params=pltpu.CompilerParams(vmem_limit_bytes=VMEM_LIMIT),
    )(place, mine, got)


def join_kernel(place_ref, *refs):
    pieces, out = refs[:Y], refs[Y]
    rows = pieces[0].shape[0]
    for k, piece in enumerate(pieces):
        start = pl.multiple_of(lax.rem(place_ref[0] + k, Y) * rows, 16)
        out[pl.ds(start, rows), :] = piece[...]


def join(pieces, place):
    rows, cols = pieces[0].shape
    return pl.pallas_call(
        join_kernel,
        out_shape=jax.ShapeDtypeStruct((Y * rows, cols), pieces[0].dtype),
        in_specs=[pl.BlockSpec(memory_space=pltpu.SMEM)] + [pl.BlockSpec(memory_space=pltpu.VMEM)] * Y,
        out_specs=pl.BlockSpec(memory_space=pltpu.VMEM),
        compiler_params=pltpu.CompilerParams(vmem_limit_bytes=VMEM_LIMIT),
    )(place, *pieces)


def products_kernel(layout, place_ref, scale_ref, *refs):
    outs_ref, refs = refs[0], refs[1:]
    chunks = len(layout)
    halves, o_ref, rows = refs[: 2 * chunks], refs[-2], refs[-1]
    z, h, core = place_ref[0], place_ref[1], place_ref[2]

    @pl.when(pl.program_id(0) == 0)
    def _():
        for n, blocks in enumerate(layout):
            for other in range(2):
                source = halves[2 * n + other]
                first = core if other == 0 else 1 - core
                count = len(blocks) // 2
                for slot in range(count):
                    low, high = blocks[slot], blocks[count + slot]
                    index = jnp.where(first == 0, low[0], high[0])
                    side = jnp.where(first == 0, low[1], high[1])
                    half = jnp.where(side == 0, h, 1 - h)
                    start = pl.multiple_of(index * LEN + half * HALF, 16)
                    rows[pl.ds(start, HALF), :] = source[slot * HALF : (slot + 1) * HALF, :]

    total = None
    for n in range(SEQS):
        product = lax.dot_general(
            outs_ref[lax.rem(z + n, SEQS), 0],
            rows[n * LEN : (n + 1) * LEN, :],
            (((0,), (0,)), ((), ())),
            preferred_element_type=jnp.float32,
        )
        total = product * product if total is None else total + product * product
    o_ref[...] = total / scale_ref[0]


def products(rotated_out, chunks, layout, place, scale):
    _, _, _, half_cols = rotated_out.shape
    in_cols = chunks[0][0].shape[1]
    tile = 512
    per = half_cols // tile
    halves = [half for chunk in chunks for half in chunk]
    smem = pl.BlockSpec(memory_space=pltpu.SMEM)
    return pl.pallas_call(
        functools.partial(products_kernel, layout),
        out_shape=jax.ShapeDtypeStruct((2 * half_cols, in_cols), jnp.float32),
        grid=(2 * per,),
        in_specs=[smem, smem, pl.BlockSpec((SEQS, 1, LEN, tile), lambda i: (0, i // per, 0, i % per))]
        + [pl.BlockSpec(half.shape, lambda i: (0, 0)) for half in halves],
        out_specs=pl.BlockSpec((tile, in_cols), lambda i: (i, 0)),
        scratch_shapes=[pltpu.VMEM((SEQS * LEN, in_cols), jnp.bfloat16)],
        compiler_params=pltpu.CompilerParams(vmem_limit_bytes=VMEM_LIMIT),
        cost_estimate=QUICK,
    )(place, scale.reshape(1), rotated_out, *halves)


def scatter_y(mine, theirs, place):
    own, *away = split_sum(mine, swap_core(theirs), place)
    return own, [shift_y(piece, k + 1) for k, piece in enumerate(away)]


def gather_y(own, came, place):
    piece = (own + came[0] + came[1] + came[2]).astype(jnp.bfloat16)
    return join([piece] + [shift_y(piece, -k) for k in (1, 2, 3)], place)


def on_device(activations, grads_out, basis_in, basis_out, lengths):
    wide, tp = lax.axis_index("wide"), lax.axis_index("tp")
    z, h = wide // 2, wide % 2
    y, core = tp // 2, tp % 2
    place, core_at = y.reshape(1), core.reshape(1)
    rows, out_cols = basis_out.shape
    half_cols = out_cols // 2

    a, c = {}, {}
    a[0] = activations
    a[-1], a[1] = shift_z(a[0], 1), shift_z(a[0], -1)
    far = swap_x(lax.dynamic_slice(basis_out, (0, (1 - h) * half_cols), (rows, half_cols)))
    near = lax.dynamic_slice(basis_out, (0, h * half_cols), (rows, half_cols))
    grads = [grads_out] + [shift_y(grads_out, -k) for k in (1, 2, 3)]
    a[-1], a[1], near, far, *grads = together(a[-1], a[1], near, far, *grads)

    a[-2], a[2] = shift_z(a[-1], 1), shift_z(a[1], -1)
    grads_near = jnp.concatenate(grads, axis=0)
    grads_far = swap_x(grads_near)
    a[-2], a[2], grads_near, grads_far = together(a[-2], a[2], grads_near, grads_far)

    a[-3], a[3], c[2] = shift_z(a[-2], 1), shift_z(a[2], -1), swap_x(a[2])
    grads = [grads_near, grads_far, swap_core(grads_near), swap_core(grads_far)]
    part = partial_out(grads, near, far, jnp.stack([y, core]))
    a[-3], a[3], c[2], part, a[1], a[-2], a[-1], a[0], basis_in = together(
        a[-3], a[3], c[2], part, a[1], a[-2], a[-1], a[0], basis_in
    )

    first = [(0, 0), (1, 0), (2, 0), (3, 0), (-1, 0), (-2, 0), (-3, 0), (2, 1)]
    second = [(4, 0), (1, 1), (0, 1), (-2, 1), (-1, 1), (3, 1), (-3, 1), (4, 1)]
    block = lambda at: (a, c)[at[1]][at[0]]
    summands = along_z(part)
    a[4], c[3] = shift_z(a[-3], 1), shift_z(c[2], -1)
    c[-2], c[1], c[0] = swap_x(a[-2]), swap_x(a[1]), swap_x(a[0])
    mine_a, theirs_a = rotate_in([block(at) for at in first], basis_in, core_at)
    a[4], c[3], c[-2], c[1], mine_a, theirs_a, a[-1], basis_in, lengths = together(
        a[4], c[3], c[-2], c[1], mine_a, theirs_a, a[-1], basis_in, lengths
    )

    c[-3], c[4], c[-1] = shift_z(c[-2], 1), shift_z(c[3], -1), swap_x(a[-1])
    token = lax.iota(jnp.int32, LEN)
    live = token < lax.dynamic_index_in_dim(lengths, z, 0, keepdims=False)
    summed = jnp.sum(summands.astype(jnp.float32), axis=0)
    summed = jnp.where(live[:, None], summed, 0.0).astype(jnp.bfloat16)
    copies = jnp.broadcast_to(summed[None], (2 * Z,) + summed.shape)
    c[-3], c[4], c[-1], c[0], copies, theirs_a = together(c[-3], c[4], c[-1], c[0], copies, theirs_a)
    rotated_out = lax.all_to_all(copies, "wide", 0, 0, tiled=True)

    own_a, came_a = scatter_y(mine_a, theirs_a, place)

    mine_b, theirs_b = rotate_in([block(at) for at in second], basis_in, core_at)
    own_b, came_b = scatter_y(mine_b, theirs_b, place)
    rows_a = gather_y(own_a, came_a, place)
    chunk_a = (rows_a, swap_core(rows_a))
    rows_b = gather_y(own_b, came_b, place)
    chunk_b = (rows_b, swap_core(rows_b))
    scale = jnp.sum(lengths).astype(jnp.float32)
    layout = [[(k % SEQS, side) for k, side in blocks] for blocks in (first, second)]
    rotated_out = rotated_out.reshape(SEQS, 2, LEN, half_cols)
    return products(rotated_out, [chunk_a, chunk_b], layout, jnp.stack([z, h, core]), scale)


def solution(mesh):
    placed = (
        P(("layer", "wide"), "tp"),
        P(("layer", "wide"), "tp"),
        P(("layer", "tp"), "wide"),
        P(("layer", "wide"), "tp"),
        P(),
    )
    return jax.shard_map(
        on_device, mesh=mesh, in_specs=placed, out_specs=P(("layer", "tp"), "wide"), check_vma=False
    )
```

```python
import functools

import jax
import jax.numpy as jnp
from jax import lax
from jax.experimental import pallas as pl
from jax.experimental.pallas import tpu as pltpu
from jax.sharding import PartitionSpec as P

LEN = 128
SEQS = 8
HALF = LEN // 2
Z = 8
Y = 4
SEND = jnp.bfloat16
ALONG_Z = [[2 * z + h for z in range(Z)] for h in range(2)]
QUICK = pl.CostEstimate(flops=1, bytes_accessed=1, transcendentals=0)
VMEM_LIMIT = 48 * 2**20


def shift_z(x, step):
    pairs = [(z * 2 + h, (z + step) % Z * 2 + h) for z in range(Z) for h in range(2)]
    return lax.ppermute(x, "wide", pairs)


def swap_x(x):
    return lax.ppermute(x, "wide", [(i, i ^ 1) for i in range(2 * Z)])


def shift_y(x, step):
    pairs = [(y * 2 + c, (y + step) % Y * 2 + c) for y in range(Y) for c in range(2)]
    return lax.ppermute(x, "tp", pairs)


def swap_core(x):
    return lax.ppermute(x, "tp", [(i, i ^ 1) for i in range(2 * Y)])


def along_z(x):
    return lax.all_to_all(x, "wide", 0, 0, tiled=True, axis_index_groups=ALONG_Z)


def together(*values):
    return lax.optimization_barrier(values)


def rotate_kernel(count, core_ref, *refs):
    blocks, basis_ref = refs[:count], refs[count]
    mine_ref, theirs_ref, total = refs[count + 1 :]
    rows = jnp.concatenate([block[...] for block in blocks], axis=0)
    term = jnp.dot(rows, basis_ref[...], preferred_element_type=jnp.float32)

    @pl.when(pl.program_id(0) == 0)
    def _():
        total[...] = term

    @pl.when(pl.program_id(0) == 1)
    def _():
        total[...] += term
        half = count * HALF // 2
        core = core_ref[0]
        mine_ref[...] = total[pl.ds(pl.multiple_of(core * half, 16), half), :]
        theirs_ref[...] = total[pl.ds(pl.multiple_of((1 - core) * half, 16), half), :]


def rotate_in(blocks, basis, core):
    count = len(blocks)
    depth, cols = basis.shape
    tile = depth // 2
    half = count * HALF // 2
    shape = jax.ShapeDtypeStruct((half, cols), jnp.float32)
    whole = pl.BlockSpec((half, cols), lambda k, core: (0, 0))
    return pl.pallas_call(
        functools.partial(rotate_kernel, count),
        out_shape=(shape, shape),
        grid_spec=pltpu.PrefetchScalarGridSpec(
            num_scalar_prefetch=1,
            grid=(2,),
            in_specs=[pl.BlockSpec((HALF, tile), lambda k, core: (0, k))] * count
            + [pl.BlockSpec((tile, cols), lambda k, core: (k, 0))],
            out_specs=(whole, whole),
            scratch_shapes=[pltpu.VMEM((count * HALF, cols), jnp.float32)],
        ),
        compiler_params=pltpu.CompilerParams(vmem_limit_bytes=VMEM_LIMIT),
        cost_estimate=QUICK,
    )(core, *blocks, basis)


def partial_kernel(place_ref, *refs):
    grads, (near_ref, far_ref, out_ref) = refs[:4], refs[4:]
    y, core = place_ref[0], place_ref[1]
    rows, cols = far_ref.shape
    own = pl.ds(pl.multiple_of(place_ref[2] * cols, 128), cols)
    lefts = []
    for near, far in (grads[:2], grads[2:]):
        for k in range(Y):
            part = pl.ds(k * rows, rows)
            lefts.append(jnp.concatenate([near[part, :], far[part, :]], axis=0))
    left = jnp.concatenate(lefts, axis=1)
    right = jnp.concatenate([near_ref[:, own], far_ref[...]], axis=0)
    term = lax.dot_general(left, right, (((0,), (0,)), ((), ())), preferred_element_type=jnp.float32)
    for n in range(SEQS):
        owner = jnp.where(n < Y, core, 1 - core)
        sequence = 2 * lax.rem(y + n % Y, Y) + owner
        out_ref[sequence] = term[n * LEN : (n + 1) * LEN, :].astype(out_ref.dtype)


def partial_out(grads, near, far, place):
    cols = far.shape[1]
    vmem = pl.BlockSpec(memory_space=pltpu.VMEM)
    return pl.pallas_call(
        partial_kernel,
        out_shape=jax.ShapeDtypeStruct((SEQS, LEN, cols), SEND),
        in_specs=[pl.BlockSpec(memory_space=pltpu.SMEM)] + [vmem] * 6,
        out_specs=vmem,
        compiler_params=pltpu.CompilerParams(vmem_limit_bytes=VMEM_LIMIT),
        cost_estimate=QUICK,
    )(place, *grads, near, far)


def split_kernel(place_ref, mine_ref, got_ref, *outs):
    rows = outs[0].shape[0]
    place = place_ref[0]
    for k, out in enumerate(outs):
        start = pl.multiple_of(lax.rem(place + k, Y) * rows, 16)
        out[...] = mine_ref[pl.ds(start, rows), :] + got_ref[pl.ds(start, rows), :]


def split_sum(mine, got, place):
    half, cols = mine.shape
    shape = jax.ShapeDtypeStruct((half // Y, cols), jnp.float32)
    return pl.pallas_call(
        split_kernel,
        out_shape=(shape,) * Y,
        in_specs=[pl.BlockSpec(memory_space=pltpu.SMEM)] + [pl.BlockSpec(memory_space=pltpu.VMEM)] * 2,
        out_specs=(pl.BlockSpec(memory_space=pltpu.VMEM),) * Y,
        compiler_params=pltpu.CompilerParams(vmem_limit_bytes=VMEM_LIMIT),
    )(place, mine, got)


def join_kernel(place_ref, *refs):
    pieces, out = refs[:Y], refs[Y]
    rows = pieces[0].shape[0]
    for k, piece in enumerate(pieces):
        start = pl.multiple_of(lax.rem(place_ref[0] + k, Y) * rows, 16)
        out[pl.ds(start, rows), :] = piece[...]


def join(pieces, place):
    rows, cols = pieces[0].shape
    return pl.pallas_call(
        join_kernel,
        out_shape=jax.ShapeDtypeStruct((Y * rows, cols), pieces[0].dtype),
        in_specs=[pl.BlockSpec(memory_space=pltpu.SMEM)] + [pl.BlockSpec(memory_space=pltpu.VMEM)] * Y,
        out_specs=pl.BlockSpec(memory_space=pltpu.VMEM),
        compiler_params=pltpu.CompilerParams(vmem_limit_bytes=VMEM_LIMIT),
    )(place, *pieces)


def products_kernel(layout, place_ref, scale_ref, *refs):
    outs_ref, refs = refs[0], refs[1:]
    chunks = len(layout)
    halves, o_ref, rows = refs[: 2 * chunks], refs[-2], refs[-1]
    z, h, core = place_ref[0], place_ref[1], place_ref[2]

    @pl.when(pl.program_id(0) == 0)
    def _():
        for n, blocks in enumerate(layout):
            for other in range(2):
                source = halves[2 * n + other]
                first = core if other == 0 else 1 - core
                count = len(blocks) // 2
                for slot in range(count):
                    low, high = blocks[slot], blocks[count + slot]
                    index = jnp.where(first == 0, low[0], high[0])
                    side = jnp.where(first == 0, low[1], high[1])
                    half = jnp.where(side == 0, h, 1 - h)
                    start = pl.multiple_of(index * LEN + half * HALF, 16)
                    rows[pl.ds(start, HALF), :] = source[slot * HALF : (slot + 1) * HALF, :]

    total = None
    for n in range(SEQS):
        product = lax.dot_general(
            outs_ref[lax.rem(z + n, SEQS), 0],
            rows[n * LEN : (n + 1) * LEN, :],
            (((0,), (0,)), ((), ())),
            preferred_element_type=jnp.float32,
        )
        total = product * product if total is None else total + product * product
    o_ref[...] = total / scale_ref[0]


def products(rotated_out, chunks, layout, place, scale):
    _, _, _, half_cols = rotated_out.shape
    in_cols = chunks[0][0].shape[1]
    tile = 512
    per = half_cols // tile
    halves = [half for chunk in chunks for half in chunk]
    smem = pl.BlockSpec(memory_space=pltpu.SMEM)
    return pl.pallas_call(
        functools.partial(products_kernel, layout),
        out_shape=jax.ShapeDtypeStruct((2 * half_cols, in_cols), jnp.float32),
        grid=(2 * per,),
        in_specs=[smem, smem, pl.BlockSpec((SEQS, 1, LEN, tile), lambda i: (0, i // per, 0, i % per))]
        + [pl.BlockSpec(half.shape, lambda i: (0, 0)) for half in halves],
        out_specs=pl.BlockSpec((tile, in_cols), lambda i: (i, 0)),
        scratch_shapes=[pltpu.VMEM((SEQS * LEN, in_cols), jnp.bfloat16)],
        compiler_params=pltpu.CompilerParams(vmem_limit_bytes=VMEM_LIMIT),
        cost_estimate=QUICK,
    )(place, scale.reshape(1), rotated_out, *halves)


def scatter_y(mine, theirs, place):
    own, *away = split_sum(mine, swap_core(theirs), place)
    return own, [shift_y(piece, k + 1) for k, piece in enumerate(away)]


def gather_y(own, came, place):
    piece = (own + came[0] + came[1] + came[2]).astype(jnp.bfloat16)
    return join([piece] + [shift_y(piece, -k) for k in (1, 2, 3)], place)


def on_device(activations, grads_out, basis_in, basis_out, lengths):
    wide, tp = lax.axis_index("wide"), lax.axis_index("tp")
    z, h = wide // 2, wide % 2
    y, core = tp // 2, tp % 2
    place, core_at = y.reshape(1), core.reshape(1)
    rows, out_cols = basis_out.shape
    half_cols = out_cols // 2

    a, c = {}, {}
    a[0] = activations
    a[-1], a[1] = shift_z(a[0], 1), shift_z(a[0], -1)
    far = swap_x(lax.dynamic_slice(basis_out, (0, (1 - h) * half_cols), (rows, half_cols)))
    grads = [grads_out] + [shift_y(grads_out, -k) for k in (1, 2, 3)]
    a[-1], a[1], far, *grads = together(a[-1], a[1], far, *grads)

    a[-2], a[2] = shift_z(a[-1], 1), shift_z(a[1], -1)
    grads_near = jnp.concatenate(grads, axis=0)
    grads_far = swap_x(grads_near)
    a[-2], a[2], grads_near, grads_far = together(a[-2], a[2], grads_near, grads_far)

    a[-3], a[3], c[2] = shift_z(a[-2], 1), shift_z(a[2], -1), swap_x(a[2])
    grads = [grads_near, grads_far, swap_core(grads_near), swap_core(grads_far)]
    part = partial_out(grads, basis_out, far, jnp.stack([y, core, h]))
    a[-3], a[3], c[2], part, a[1], a[-2], a[-1], a[0], basis_in = together(
        a[-3], a[3], c[2], part, a[1], a[-2], a[-1], a[0], basis_in
    )

    first = [(0, 0), (1, 0), (2, 0), (3, 0), (-1, 0), (-2, 0), (-3, 0), (2, 1)]
    second = [(4, 0), (1, 1), (0, 1), (-2, 1), (-1, 1), (3, 1), (-3, 1), (4, 1)]
    block = lambda at: (a, c)[at[1]][at[0]]
    summands = along_z(part)
    a[4], c[3] = shift_z(a[-3], 1), shift_z(c[2], -1)
    c[-2], c[1], c[0] = swap_x(a[-2]), swap_x(a[1]), swap_x(a[0])
    mine_a, theirs_a = rotate_in([block(at) for at in first], basis_in, core_at)
    a[4], c[3], c[-2], c[1], mine_a, theirs_a, a[-1], basis_in, lengths = together(
        a[4], c[3], c[-2], c[1], mine_a, theirs_a, a[-1], basis_in, lengths
    )

    c[-3], c[4], c[-1] = shift_z(c[-2], 1), shift_z(c[3], -1), swap_x(a[-1])
    token = lax.iota(jnp.int32, LEN)
    live = token < lax.dynamic_index_in_dim(lengths, z, 0, keepdims=False)
    summed = jnp.sum(summands.astype(jnp.float32), axis=0)
    summed = jnp.where(live[:, None], summed, 0.0).astype(jnp.bfloat16)
    copies = jnp.broadcast_to(summed[None], (2 * Z,) + summed.shape)
    c[-3], c[4], c[-1], c[0], copies, theirs_a = together(c[-3], c[4], c[-1], c[0], copies, theirs_a)
    rotated_out = lax.all_to_all(copies, "wide", 0, 0, tiled=True)

    own_a, came_a = scatter_y(mine_a, theirs_a, place)

    mine_b, theirs_b = rotate_in([block(at) for at in second], basis_in, core_at)
    own_b, came_b = scatter_y(mine_b, theirs_b, place)
    rows_a = gather_y(own_a, came_a, place)
    chunk_a = (rows_a, swap_core(rows_a))
    rows_b = gather_y(own_b, came_b, place)
    chunk_b = (rows_b, swap_core(rows_b))
    scale = jnp.sum(lengths).astype(jnp.float32)
    layout = [[(k % SEQS, side) for k, side in blocks] for blocks in (first, second)]
    rotated_out = rotated_out.reshape(SEQS, 2, LEN, half_cols)
    return products(rotated_out, [chunk_a, chunk_b], layout, jnp.stack([z, h, core]), scale)


def solution(mesh):
    placed = (
        P(("layer", "wide"), "tp"),
        P(("layer", "wide"), "tp"),
        P(("layer", "tp"), "wide"),
        P(("layer", "wide"), "tp"),
        P(),
    )
    return jax.shard_map(
        on_device, mesh=mesh, in_specs=placed, out_specs=P(("layer", "tp"), "wide"), check_vma=False
    )
```
